256 devices in a mesh: row: 8 (over z_lo, y), col: 32 (over z_hi, x, core).
Axes of the slice: x: 4, y: 4, z: 8 (z_hi: 4, z_lo: 2; z = z_hi * 2 + z_lo), core: 2. Of those that a mesh axis runs over, the one named last changes fastest.
Arguments:
- activations: bfloat16 [1024, 8192], P('col', 'row'), may hold values from -6 to 6
- cotangent: bfloat16 [1024, 8192], P('col', 'row'), may hold values from -0.59765625 to 0.59765625
- gate_weight: bfloat16 [8192, 21504], P('row', 'col'), may hold values from -0.0625 to 0.0625
- up_weight: bfloat16 [8192, 21504], P('row', 'col'), may hold values from -0.0625 to 0.0625
- down_weight: bfloat16 [21504, 8192], P('col', 'row'), may hold values from -0.0390625 to 0.0390625
Outputs:
- input_grad: bfloat16 [1024, 8192], P('col', 'row')
- gate_grad: bfloat16 [8192, 21504], P('row', 'col')
- up_grad: bfloat16 [8192, 21504], P('row', 'col')
- down_grad: bfloat16 [21504, 8192], P('col', 'row')
The draws below stay inside these ranges and needn't reach their ends.
All inputs are finite; a program needn't handle non-finite values.
Results may differ from the reference program's by a relative error of at most 0.005.
Values may be sent and summed in bfloat16 or wider, within the bound.
No kernel may reach another device: no remote copies, remote signals or barrier semaphores. Data moves between devices by JAX's collectives and lax.ppermute only.
A program may use at most 128 MiB of HBM per device.

```python
import jax
import jax.numpy as jnp
from jax import lax

D = 8192
FF = 21504
TOKENS = 1024


def levels(key, dims, cuts, low, top_value):
    def one(axis_at, parts):
        draws = jax.random.uniform(jax.random.fold_in(jax.random.fold_in(key, 6), axis_at), (parts,), jnp.float32, low / len(cuts), top_value / len(cuts))
        return jnp.repeat(jnp.exp(draws), dims[axis_at] // parts).reshape((-1,) + (1,) * (len(dims) - axis_at - 1))

    level = one(*cuts[0])
    for cut in cuts[1:]:
        level = level * one(*cut)
    return level


def normal_values(rng, dims, width, reach, cuts=(), dtype=jnp.bfloat16):
    result = jax.random.normal(rng, dims, jnp.float32) * width
    if len(cuts) > 0:
        result = levels(rng, dims, cuts, -0.22, 0.18) * result
    return jnp.clip(result, min=-reach, max=reach).astype(dtype)


def setup_inputs(seed: int = 0) -> dict:
    key_of = jax.random.split(jax.random.key(seed), 6)
    return {
        "activations": normal_values(key_of[0], (TOKENS, D), 1.0, 6.0, ((0, 32), (1, 8))),
        "cotangent": normal_values(key_of[1], (TOKENS, D), 0.1, 0.59765625, ((0, 32), (1, 8))),
        "gate_weight": normal_values(key_of[2], (D, FF), D ** -0.5, 0.0625, ((0, 8), (1, 32))),
        "up_weight": normal_values(key_of[3], (D, FF), D ** -0.5, 0.0625, ((0, 8), (1, 32))),
        "down_weight": normal_values(key_of[4], (FF, D), FF ** -0.5, 0.0390625, ((0, 32), (1, 8))),
    }


def reference(activations, cotangent, gate_weight, up_weight, down_weight):
    gate = jnp.dot(activations, gate_weight, preferred_element_type=jnp.float32)
    up = jnp.dot(activations, up_weight, preferred_element_type=jnp.float32)
    hidden_grad = lax.dot_general(cotangent, down_weight, (((1,), (1,)), ((), ())), preferred_element_type=jnp.float32)
    sigmoid_gate = jax.nn.sigmoid(gate)
    hidden = (gate * sigmoid_gate * up).astype(jnp.bfloat16)
    gate_delta = (hidden_grad * up * sigmoid_gate * (1.0 + gate * (1.0 - sigmoid_gate))).astype(jnp.bfloat16)
    up_delta = (hidden_grad * gate * sigmoid_gate).astype(jnp.bfloat16)
    contract_rows = (((0,), (0,)), ((), ()))
    down_grad = lax.dot_general(hidden, cotangent, contract_rows, preferred_element_type=jnp.float32).astype(jnp.bfloat16)
    gate_grad = lax.dot_general(activations, gate_delta, contract_rows, preferred_element_type=jnp.float32).astype(jnp.bfloat16)
    up_grad = lax.dot_general(activations, up_delta, contract_rows, preferred_element_type=jnp.float32).astype(jnp.bfloat16)
    contract_cols = (((1,), (1,)), ((), ()))
    input_grad = lax.dot_general(gate_delta, gate_weight, contract_cols, preferred_element_type=jnp.float32)
    input_grad = input_grad + lax.dot_general(up_delta, up_weight, contract_cols, preferred_element_type=jnp.float32)
    return input_grad.astype(jnp.bfloat16), gate_grad, up_grad, down_grad
```

```python
import functools

import jax
import jax.numpy as jnp
from jax import lax
from jax.experimental import pallas as pl
from jax.experimental.pallas import tpu as pltpu
from jax.sharding import PartitionSpec as P

BF16, F32 = jnp.bfloat16, jnp.float32
NY, NZH, NX = 4, 4, 4
CHUNKS = ((0, 1), (2, 3))
RS_RING = False
AG_RING = False
C_DTYPE = BF16
ZH_DTYPE = BF16

NT = (((1,), (1,)), ((), ()))
NN = (((1,), (0,)), ((), ()))
TN = (((0,), (0,)), ((), ()))


def dot(a, b, dims):
    return lax.dot_general(a, b, dims, preferred_element_type=F32)


def shift_y(v, k):
    return lax.ppermute(v, "row", [(z * NY + y, z * NY + (y + k) % NY) for z in range(2) for y in range(NY)])


def swap_zl(v):
    return lax.ppermute(v, "row", [(r, (r + NY) % (2 * NY)) for r in range(2 * NY)])


def shift_col(v, dzh=0, dx=0, dc=0):
    pairs = []
    for zh in range(NZH):
        for x in range(NX):
            for c in range(2):
                at = (zh * NX + x) * 2 + c
                to = (((zh + dzh) % NZH) * NX + (x + dx) % NX) * 2 + (c + dc) % 2
                pairs.append((at, to))
    return lax.ppermute(v, "col", pairs)


def cost(flops, bytes_accessed):
    return pl.CostEstimate(flops=int(flops), bytes_accessed=int(bytes_accessed), transcendentals=0)


def nbytes(*arrays):
    return sum(a.size * a.dtype.itemsize for a in arrays)


def call(kernel, y, inputs, specs, outs, flops, name):
    return pl.pallas_call(
        kernel,
        out_shape=outs,
        grid_spec=pltpu.PrefetchScalarGridSpec(
            num_scalar_prefetch=1,
            grid=(1,),
            in_specs=specs,
            out_specs=[whole(o) for o in outs],
        ),
        compiler_params=pltpu.CompilerParams(vmem_limit_bytes=56 * 2**20),
        cost_estimate=cost(flops, nbytes(*inputs, *outs)),
        name=name,
    )(y, *inputs)


def whole(a):
    return pl.BlockSpec(a.shape, lambda i, y, n=len(a.shape): (0,) * n)


def weight_block(w, k):
    return pl.BlockSpec((1,) + w.shape[1:], lambda i, y: ((y[0] + k) % NY, 0, 0))


def partial_kernel(ks, adds, n_adds, y_ref, *refs):
    halves, refs = refs[:2], refs[2:]
    weights, refs = refs[: 3 * len(ks)], refs[3 * len(ks) :]
    added, outs = refs[:n_adds], refs[n_adds:]
    for i in range(len(ks)):
        for h in range(2):
            for m in range(3):
                part = dot(weights[3 * i + m][0], halves[h][1 if m == 2 else 0], NT)
                for at, half in adds[i]:
                    if half is None:
                        part = part + added[at][h, m].astype(F32)
                    elif half == h:
                        part = part + added[at][m].astype(F32)
                outs[i][h, m] = part.astype(outs[i].dtype)


def partials(y, halves, weights, ks, adds, added, dtype, name):
    rows, tokens = weights[0].shape[1], halves[0].shape[1]
    outs = [jax.ShapeDtypeStruct((2, 3, rows, tokens), dtype) for _ in ks]
    specs = [whole(h) for h in halves]
    inputs = list(halves)
    for k in ks:
        for w in weights:
            inputs.append(w)
            specs.append(weight_block(w, k))
    for a in added:
        inputs.append(a)
        specs.append(whole(a))
    flops = 2 * len(ks) * 6 * rows * tokens * weights[0].shape[2]
    return call(functools.partial(partial_kernel, ks, adds, len(added)), y, inputs, specs, outs, flops, name)


def deltas(sums):
    gate, up, hidden_grad = sums[:, 0], sums[:, 1], sums[:, 2]
    s = jax.nn.sigmoid(gate)
    hidden = (gate * s * up).astype(BF16)
    gate_delta = (hidden_grad * up * s * (1.0 + gate * (1.0 - s))).astype(BF16)
    up_delta = (hidden_grad * gate * s).astype(BF16)
    return jnp.stack([hidden, gate_delta, up_delta], axis=1)


def delta_at(group, k, h, m):
    if k == 2 and len(group) == 5:
        return group[2 + h][m]
    return group[k if k < 3 else len(group) - 1][h, m]


def input_kernel(n, y_ref, gate_ref, up_ref, *refs):
    group, (own, other) = refs[:n], refs[n:]
    for h, out in ((0, own), (1, other)):
        total = None
        for k in range(NY):
            block = lax.rem(y_ref[0] + NY - k, NY)
            for m, w in ((1, gate_ref), (2, up_ref)):
                term = dot(delta_at(group, k, h, m), w[block], TN)
                total = term if total is None else total + term
        out[...] = total.astype(out.dtype)


def input_part(y, gate_w, up_w, group):
    tokens, feats = group[0].shape[-1], gate_w.shape[2]
    outs = [jax.ShapeDtypeStruct((tokens, feats), F32), jax.ShapeDtypeStruct((tokens, feats), C_DTYPE)]
    inputs = [gate_w, up_w, *group]
    flops = 2 * 2 * tokens * 2 * NY * gate_w.shape[1] * feats
    return call(functools.partial(input_kernel, len(group)), y, inputs, [whole(a) for a in inputs], outs, flops, "input_part")


def grads_kernel(layout, y_ref, *refs):
    n = sum(2 + g for g in layout)
    ins, (down, gate, up) = refs[:n], refs[n:]
    chunks, at = [], 0
    for g in layout:
        chunks.append((ins[at : at + 2], ins[at + 2 : at + 2 + g]))
        at += 2 + g
    for k in range(NY):
        block = lax.rem(y_ref[0] + NY - k, NY)
        for m, out in ((0, down), (1, gate), (2, up)):
            total = None
            for halves, group in chunks:
                for h in range(2):
                    term = dot(delta_at(group, k, h, m), halves[h][1 if m == 0 else 0], NN)
                    total = term if total is None else total + term
            out[block] = total.astype(out.dtype)


def weight_grads(y, chunks, shape):
    inputs, layout = [], []
    for halves, group in chunks:
        inputs += [*halves, *group]
        layout.append(len(group))
    outs = [jax.ShapeDtypeStruct(shape, BF16)] * 3
    tokens = sum(2 * h[0].shape[1] for h, _ in chunks)
    flops = 2 * 3 * tokens * shape[0] * shape[1] * shape[2]
    return call(functools.partial(grads_kernel, layout), y, inputs, [whole(a) for a in inputs], outs, flops, "weight_grads")


def per_device(activations, cotangent, gate_weight, up_weight, down_weight):
    y = lax.rem(lax.axis_index("row"), NY)[None].astype(jnp.int32)
    rows, feats = activations.shape
    hid = gate_weight.shape[1]
    shape = (NY, hid // NY, feats)
    weights = [w.reshape(shape) for w in (gate_weight.T, up_weight.T, down_weight)]

    both = jnp.stack([activations, cotangent])
    mine = jnp.stack([both] + [shift_col(both, dzh=k) for k in range(1, NZH)], axis=1)
    mine = mine.reshape(2, NZH * rows, feats)
    moved = {s: shift_col(mine, dx=s) if s else mine for s in sum(CHUNKS, ())}

    done, input_sums = [], None
    for chunk in CHUNKS:
        own = jnp.concatenate([moved[s] for s in chunk], axis=1) if len(chunk) > 1 else moved[chunk[0]]
        halves = (own, shift_col(own, dc=1))
        if RS_RING:
            (far,) = partials(y, halves, weights, (2,), ((),), (), BF16, "partial_far")
            a, b = shift_y(far[0], 1), shift_y(far[1], -1)
            right, left = partials(y, halves, weights, (1, 3), (((0, 0),), ((1, 1),)), (a, b), BF16, "partial_near")
            arrived = [shift_y(right, 1), shift_y(left, -1)]
        else:
            out = partials(y, halves, weights, (2, 1, 3), ((), (), ()), (), BF16, "partial_sent")
            arrived = [shift_y(v, k) for v, k in zip(out, (2, 1, -1))]
        (sums,) = partials(y, halves, weights, (0,), (tuple((i, None) for i in range(len(arrived))),), arrived, F32, "partial_own")
        d0 = deltas(sums + swap_zl(sums))
        d1, d3 = shift_y(d0, 1), shift_y(d0, -1)
        if AG_RING:
            group = (d0, d1, shift_y(d1[0], 1), shift_y(d3[1], -1), d3)
        else:
            group = (d0, d1, shift_y(d0, 2), d3)
        done.append((halves, group))

        keep, send = input_part(y, weights[0], weights[1], group)
        pair = keep + shift_col(send, dc=1).astype(F32)
        pair = pair.reshape(len(chunk), NZH * rows, feats)
        for i, s in enumerate(chunk):
            part = shift_col(pair[i].astype(BF16), dx=-s).astype(F32) if s else pair[i]
            input_sums = part if input_sums is None else input_sums + part

    input_sums = input_sums.reshape(NZH, rows, feats)
    input_grad = input_sums[0]
    for k in range(1, NZH):
        input_grad = input_grad + shift_col(input_sums[k].astype(ZH_DTYPE), dzh=-k).astype(F32)
    down_grad, gate_grad, up_grad = weight_grads(y, done, shape)
    return (
        input_grad.astype(BF16),
        gate_grad.reshape(hid, feats).T,
        up_grad.reshape(hid, feats).T,
        down_grad.reshape(hid, feats),
    )


def solution(mesh):
    return jax.shard_map(
        per_device,
        mesh=mesh,
        in_specs=(P("col", "row"), P("col", "row"), P("row", "col"), P("row", "col"), P("col", "row")),
        out_specs=(P("col", "row"), P("row", "col"), P("row", "col"), P("col", "row")),
        check_vma=False,
    )
```

```python
import functools

import jax
import jax.numpy as jnp
from jax import lax
from jax.experimental import pallas as pl
from jax.experimental.pallas import tpu as pltpu
from jax.sharding import PartitionSpec as P


BF16, F32 = jnp.bfloat16, jnp.float32
NY, NZH, NX = 4, 4, 4
CHUNKS = ((0,), (1, 3), (2,))
GROUPS = ((0,), (1,), (2,))
AHEAD = {1: (2,)}
ZL_AHEAD = {}
AG_RING = (True, True, False)
ZL_DTYPE = (F32, BF16, BF16)
VMEM_MB = 10
ORDER = (
    "f0", "s0", "f1", "o0", "s1", "f2", "d0", "o1", "s2", "d1",
    "o2", "i0", "p0", "d2", "i1", "i2", "p1", "p2", "w", "z",
)
ZH_DTYPE = BF16

NT = (((1,), (1,)), ((), ()))
NN = (((1,), (0,)), ((), ()))
TN = (((0,), (0,)), ((), ()))


def dot(a, b, dims):
    return lax.dot_general(a, b, dims, preferred_element_type=F32)


def shift_y(v, k):
    return lax.ppermute(v, "row", [(z * NY + y, z * NY + (y + k) % NY) for z in range(2) for y in range(NY)])


def swap_zl(v):
    return lax.ppermute(v, "row", [(r, (r + NY) % (2 * NY)) for r in range(2 * NY)])


def shift_col(v, dzh=0, dx=0, dc=0):
    pairs = []
    for zh in range(NZH):
        for x in range(NX):
            for c in range(2):
                at = (zh * NX + x) * 2 + c
                to = (((zh + dzh) % NZH) * NX + (x + dx) % NX) * 2 + (c + dc) % 2
                pairs.append((at, to))
    return lax.ppermute(v, "col", pairs)


HEAVY = 10e9
LONG = ("own", "input2")


def cost(flops, bytes_accessed):
    return pl.CostEstimate(flops=int(flops), bytes_accessed=int(bytes_accessed), transcendentals=0)


def nbytes(*arrays):
    return sum(a.size * a.dtype.itemsize for a in arrays)


class Line:
    def __init__(self):
        self.last = None

    def call(self, kernel, inputs, outs, flops, name, scalars=(), after=(), vmem=VMEM_MB):
        flops = HEAVY if name.startswith(LONG) else 0
        after = list(after) + ([self.last] if self.last is not None else [])
        n_s, n_a = len(scalars), len(after)

        def run(*refs):
            kernel(*refs[:n_s], *refs[n_s + n_a :])

        vm = pl.BlockSpec(memory_space=pltpu.VMEM)
        res = pl.pallas_call(
            run,
            out_shape=outs,
            in_specs=[pl.BlockSpec(memory_space=pltpu.SMEM)] * n_s + [pl.BlockSpec(memory_space=pl.ANY)] * n_a + [vm] * len(inputs),
            out_specs=[vm] * len(outs),
            compiler_params=pltpu.CompilerParams(vmem_limit_bytes=vmem * 2**20),
            cost_estimate=cost(flops, 0),
            name=name,
        )(*scalars, *after, *inputs)
        self.last = res[0]
        return res


def sds(shape, dtype):
    return jax.ShapeDtypeStruct(shape, dtype)


def pack_kernel(copied, *refs):
    ins, outs = refs[: -1 - copied], refs[-1 - copied :]
    if copied:
        outs[1][...] = ins[-1][...]
        ins = ins[:-1]
    at = 0
    for r in ins:
        size = r.shape[1]
        outs[0][:, at : at + size] = r[...]
        at += size


def pair_kernel(keep, got, *outs):
    rows = outs[0].shape[0]
    for j, out in enumerate(outs):
        at = slice(j * rows, (j + 1) * rows)
        out[...] = (keep[at] + got[at]).astype(out.dtype)


def sum_kernel(*refs):
    total = refs[0][...].astype(F32)
    for p in refs[1:-1]:
        total = total + p[...].astype(F32)
    refs[-1][...] = total


def total_kernel(*refs):
    parts, outs = refs[: -NZH], refs[-NZH:]
    rows = outs[0].shape[0]
    for k, out in enumerate(outs):
        at = slice(k * rows, (k + 1) * rows)
        total = parts[0][at].astype(F32)
        for p in parts[1:]:
            total = total + p[at].astype(F32)
        out[...] = total.astype(out.dtype)


def block_part(block, gu_ref, dn_ref, half):
    gate_up = dot(gu_ref[block], half[0], NT)
    down = dot(dn_ref[block], half[1], NT)
    return jnp.concatenate([gate_up, down], axis=0)


def sent_kernel(y_ref, gu_ref, dn_ref, own, other, *outs):
    for out, k in zip(outs, (2, 1, 3)):
        block = lax.rem(y_ref[0] + k, NY)
        for h, half in enumerate((own, other)):
            out[h] = block_part(block, gu_ref, dn_ref, half).astype(out.dtype)


def own_kernel(y_ref, gu_ref, dn_ref, own, other, a, b, c, out, *sent):
    for h, half in enumerate((own, other)):
        part = block_part(y_ref[0], gu_ref, dn_ref, half)
        part = part + a[h].astype(F32) + b[h].astype(F32) + c[h].astype(F32)
        out[h] = part
        for s in sent:
            s[h] = part.astype(s.dtype)


def delta_kernel(*refs):
    ins, out = refs[:-1], refs[-1]
    at = 0
    for mine, theirs in zip(ins[::2], ins[1::2]):
        rows, size = mine.shape[1] // 3, mine.shape[2]
        for h in range(2):
            sums = mine[h] + theirs[h].astype(F32)
            gate, up, hidden_grad = sums[:rows], sums[rows : 2 * rows], sums[2 * rows :]
            s = 1.0 / (1.0 + jnp.exp(-gate))
            silu = gate * s
            gate_delta = hidden_grad * up * s * (1.0 + gate * (1.0 - s))
            three = jnp.concatenate([gate_delta, hidden_grad * silu, silu * up], axis=0)
            out[h, :, at : at + size] = three.astype(out.dtype)
        at += size


def delta_at(group, k, h):
    if k == 2 and len(group) == 5:
        return group[2 + h]
    return group[k if k < 3 else len(group) - 1].at[h]


def input_kernel(y_ref, gu_ref, *refs):
    group, (own, other) = refs[:-2], refs[-2:]
    for h, out in ((0, own), (1, other)):
        total = None
        for k in range(NY):
            block = lax.rem(y_ref[0] + NY - k, NY)
            term = dot(delta_at(group, k, h)[: gu_ref.shape[1]], gu_ref[block], TN)
            total = term if total is None else total + term
        out[...] = total.astype(out.dtype)


def grads_kernel(layout, y_ref, *refs):
    ins, (gate, up, down) = list(refs[:-3]), refs[-3:]
    rows = gate.shape[1]
    groups = []
    for n_chunks, n_parts in layout:
        halves = [(ins.pop(0), ins.pop(0)) for _ in range(n_chunks)]
        groups.append((halves, [ins.pop(0) for _ in range(n_parts)]))
    for k in range(NY):
        block = lax.rem(y_ref[0] + NY - k, NY)
        gate_up, dn = None, None
        for halves, group in groups:
            for h in range(2):
                d = delta_at(group, k, h)
                at = 0
                for pair in halves:
                    tokens = slice(at, at + pair[h].shape[1])
                    at = tokens.stop
                    t = dot(d[: 2 * rows, tokens], pair[h][0], NN)
                    gate_up = t if gate_up is None else gate_up + t
                    t = dot(d[2 * rows :, tokens], pair[h][1], NN)
                    dn = t if dn is None else dn + t
        gate[block] = gate_up[:rows].astype(gate.dtype)
        up[block] = gate_up[rows:].astype(up.dtype)
        down[block] = dn.astype(down.dtype)


def per_device(activations, cotangent, gate_weight, up_weight, down_weight):
    y = lax.rem(lax.axis_index("row"), NY)[None].astype(jnp.int32)
    rows, feats = activations.shape
    hid = gate_weight.shape[1]
    hb = hid // NY
    shape = (NY, hb, feats)
    gate_up_w = jnp.concatenate([gate_weight.T.reshape(shape), up_weight.T.reshape(shape)], axis=1)
    down_w = down_weight.reshape(shape)
    line = Line()
    zh_tokens = NZH * rows
    n = len(CHUNKS)

    both = jnp.stack([activations, cotangent])
    gathered = [both] + [shift_col(both, dzh=k) for k in range(1, NZH)]
    source = line.call(functools.partial(pack_kernel, False), gathered, [sds((2, zh_tokens, feats), BF16)], 0, "pack_zh")[0]
    moved, halves, sent, sums, other_sums, groups = {0: source}, {}, {}, {}, {}, {}
    inputs, parts, final = {}, [], None

    def fetch_x(i, source):
        for s in CHUNKS[i]:
            if s not in moved:
                moved[s] = shift_col(source, dx=s)

    for what in ORDER:
        kind, i = what[0], int(what[1:] or 0)
        th = len(CHUNKS[i]) * zh_tokens if kind in "fso" else 0
        if kind == "f":
            pieces = [moved[s] for s in CHUNKS[i]]
            own = pieces[0]
            if len(pieces) > 1 or 0 < i < n - 1:
                out = [sds((2, th, feats), BF16)] + [sds(source.shape, BF16)] * (i < n - 1)
                res = line.call(functools.partial(pack_kernel, i < n - 1), pieces + [source] * (i < n - 1), out, 0, f"pack_x{i}")
                own, source = res[0], res[-1]
            halves[i] = (own, shift_col(own, dc=1))
            if i < n - 1:
                fetch_x(i + 1, source)
        elif kind == "s":
            ins = [gate_up_w, down_w, *halves[i]]
            out = [sds((2, 3 * hb, th), BF16)] * 3
            res = line.call(sent_kernel, ins, out, 2 * 9 * hb * 2 * th * feats, f"sent{i}", (y,))
            sent[i] = [shift_y(v, k) for v, k in zip(res, (2, 1, -1))]
        elif kind == "o":
            ins = [gate_up_w, down_w, *halves[i], *sent[i]]
            out = [sds((2, 3 * hb, th), F32)]
            if ZL_DTYPE[i] != F32:
                out.append(sds((2, 3 * hb, th), ZL_DTYPE[i]))
            after = [other_sums[j] for j in ZL_AHEAD.get(i, ())]
            res = line.call(own_kernel, ins, out, 2 * 3 * hb * 2 * th * feats, f"own{i}", (y,), after)
            sums[i], other_sums[i] = res[0], swap_zl(res[-1])
        elif kind == "d":
            ins = sum([[sums[j], other_sums[j]] for j in GROUPS[i]], [])
            th = sum(v.shape[2] for v in ins[::2])
            d0 = line.call(delta_kernel, ins, [sds((2, 3 * hb, th), BF16)], 0, f"delta{i}")[0]
            d1, d3 = shift_y(d0, 1), shift_y(d0, -1)
            if AG_RING[i]:
                groups[i] = (d0, d1, shift_y(d1[0], 1), shift_y(d3[1], -1), d3)
            else:
                groups[i] = (d0, d1, shift_y(d0, 2), d3)
        elif kind == "i":
            ins = [gate_up_w, *groups[i]]
            th = groups[i][0].shape[2]
            after = [groups[j][-1] for j in AHEAD.get(i, ())]
            out = [sds((th, feats), F32)] * 2
            keep, send = line.call(input_kernel, ins, out, 2 * 4 * hid * th * feats, f"input{i}", (y,), after)
            inputs[i] = (keep, shift_col(send, dc=1))
        elif kind == "p":
            shifts = sum([CHUNKS[j] for j in GROUPS[i]], ())
            out = [sds((zh_tokens, feats), BF16 if s else F32) for s in shifts]
            res = line.call(pair_kernel, inputs[i], out, 0, f"pair{i}")
            parts += [shift_col(v, dx=-s) if s else v for v, s in zip(res, shifts)]
        elif kind == "t":
            parts = [line.call(sum_kernel, parts, [sds((zh_tokens, feats), F32)], 0, "input_early")[0]]
        elif kind == "z":
            out = [sds((rows, feats), F32)] + [sds((rows, feats), ZH_DTYPE)] * (NZH - 1)
            res = line.call(total_kernel, parts, out, 0, "input_total")
            final = res[0]
            for k in range(1, NZH):
                final = final + shift_col(res[k], dzh=-k).astype(F32)
        elif kind == "w":
            ins, layout = [], []
            for j, chunks in enumerate(GROUPS):
                for c in chunks:
                    ins += halves[c]
                ins += groups[j]
                layout.append((len(chunks), len(groups[j])))
            flops = 2 * 3 * NZH * NX * 2 * rows * hid * feats
            gate_grad, up_grad, down_grad = line.call(
                functools.partial(grads_kernel, layout), ins, [sds(shape, BF16)] * 3, flops, "weight_grads", (y,)
            )
    return (
        final.astype(BF16),
        gate_grad.reshape(hid, feats).T,
        up_grad.reshape(hid, feats).T,
        down_grad.reshape(hid, feats),
    )


def solution(mesh):
    return jax.shard_map(
        per_device,
        mesh=mesh,
        in_specs=(P("col", "row"), P("col", "row"), P("row", "col"), P("row", "col"), P("col", "row")),
        out_specs=(P("col", "row"), P("row", "col"), P("row", "col"), P("col", "row")),
        check_vma=False,
    )
```

```python
import functools

import jax
import jax.numpy as jnp
from jax import lax
from jax.experimental import pallas as pl
from jax.experimental.pallas import tpu as pltpu
from jax.sharding import PartitionSpec as P


BF16, F32 = jnp.bfloat16, jnp.float32
NY, NZH, NX = 4, 4, 4
CHUNKS = ((0,), (1, 3), (2,))
GROUPS = ((0,), (1,), (2,))
EARLY_GROUPS, LATE_GROUPS = (1, 2), (0,)
AHEAD = {1: (2,), 2: (0,)}
ZL_AHEAD = {1: (0,)}
AG_RING = (False, True, False)
ZL_DTYPE = (F32, BF16, BF16)
VMEM_MB = 10
ORDER = (
    "f0", "s0", "f1", "o0", "s1", "f2", "o1", "s2", "d1", "o2",
    "d2", "d0", "i1", "i2", "p1", "p2", "v", "t", "i0", "p0", "z",
    "w",
)
ZH_DTYPE = BF16

NT = (((1,), (1,)), ((), ()))
NN = (((1,), (0,)), ((), ()))
TN = (((0,), (0,)), ((), ()))


def dot(a, b, dims):
    return lax.dot_general(a, b, dims, preferred_element_type=F32)


def shift_y(v, k):
    return lax.ppermute(v, "row", [(z * NY + y, z * NY + (y + k) % NY) for z in range(2) for y in range(NY)])


def swap_zl(v):
    return lax.ppermute(v, "row", [(r, (r + NY) % (2 * NY)) for r in range(2 * NY)])


def shift_col(v, dzh=0, dx=0, dc=0):
    pairs = []
    for zh in range(NZH):
        for x in range(NX):
            for c in range(2):
                at = (zh * NX + x) * 2 + c
                to = (((zh + dzh) % NZH) * NX + (x + dx) % NX) * 2 + (c + dc) % 2
                pairs.append((at, to))
    return lax.ppermute(v, "col", pairs)


HEAVY = 10e9
LONG = ("own", "input0", "input2")


def cost(flops, bytes_accessed):
    return pl.CostEstimate(flops=int(flops), bytes_accessed=int(bytes_accessed), transcendentals=0)


def nbytes(*arrays):
    return sum(a.size * a.dtype.itemsize for a in arrays)


class Line:
    def __init__(self):
        self.last = None

    def call(self, kernel, inputs, outs, flops, name, scalars=(), after=(), vmem=VMEM_MB):
        flops = HEAVY if name.startswith(LONG) else 0
        after = list(after) + ([self.last] if self.last is not None else [])
        n_s, n_a = len(scalars), len(after)

        def run(*refs):
            kernel(*refs[:n_s], *refs[n_s + n_a :])

        vm = pl.BlockSpec(memory_space=pltpu.VMEM)
        res = pl.pallas_call(
            run,
            out_shape=outs,
            in_specs=[pl.BlockSpec(memory_space=pltpu.SMEM)] * n_s + [pl.BlockSpec(memory_space=pl.ANY)] * n_a + [vm] * len(inputs),
            out_specs=[vm] * len(outs),
            compiler_params=pltpu.CompilerParams(vmem_limit_bytes=vmem * 2**20),
            cost_estimate=cost(flops, 0),
            name=name,
        )(*scalars, *after, *inputs)
        self.last = res[0]
        return res


def sds(shape, dtype):
    return jax.ShapeDtypeStruct(shape, dtype)


def pack_kernel(copied, *refs):
    ins, outs = refs[: -1 - copied], refs[-1 - copied :]
    if copied:
        outs[1][...] = ins[-1][...]
        ins = ins[:-1]
    at = 0
    for r in ins:
        size = r.shape[1]
        outs[0][:, at : at + size] = r[...]
        at += size


def pair_kernel(keep, got, *outs):
    rows = outs[0].shape[0]
    for j, out in enumerate(outs):
        at = slice(j * rows, (j + 1) * rows)
        out[...] = (keep[at] + got[at]).astype(out.dtype)


def sum_kernel(*refs):
    total = refs[0][...].astype(F32)
    for p in refs[1:-1]:
        total = total + p[...].astype(F32)
    refs[-1][...] = total


def total_kernel(*refs):
    parts, outs = refs[: -NZH], refs[-NZH:]
    rows = outs[0].shape[0]
    for k, out in enumerate(outs):
        at = slice(k * rows, (k + 1) * rows)
        total = parts[0][at].astype(F32)
        for p in parts[1:]:
            total = total + p[at].astype(F32)
        out[...] = total.astype(out.dtype)


def block_part(block, gu_ref, dn_ref, half):
    gate_up = dot(gu_ref[block], half[0], NT)
    down = dot(dn_ref[block], half[1], NT)
    return jnp.concatenate([gate_up, down], axis=0)


def sent_kernel(y_ref, gu_ref, dn_ref, own, other, *outs):
    for out, k in zip(outs, (2, 1, 3)):
        block = lax.rem(y_ref[0] + k, NY)
        for h, half in enumerate((own, other)):
            out[h] = block_part(block, gu_ref, dn_ref, half).astype(out.dtype)


def own_kernel(y_ref, gu_ref, dn_ref, own, other, a, b, c, out, *sent):
    for h, half in enumerate((own, other)):
        part = block_part(y_ref[0], gu_ref, dn_ref, half)
        part = part + a[h].astype(F32) + b[h].astype(F32) + c[h].astype(F32)
        out[h] = part
        for s in sent:
            s[h] = part.astype(s.dtype)


def delta_kernel(*refs):
    ins, out = refs[:-1], refs[-1]
    at = 0
    for mine, theirs in zip(ins[::2], ins[1::2]):
        rows, size = mine.shape[1] // 3, mine.shape[2]
        for h in range(2):
            sums = mine[h] + theirs[h].astype(F32)
            gate, up, hidden_grad = sums[:rows], sums[rows : 2 * rows], sums[2 * rows :]
            s = 1.0 / (1.0 + jnp.exp(-gate))
            silu = gate * s
            gate_delta = hidden_grad * up * s * (1.0 + gate * (1.0 - s))
            three = jnp.concatenate([gate_delta, hidden_grad * silu, silu * up], axis=0)
            out[h, :, at : at + size] = three.astype(out.dtype)
        at += size


def delta_at(group, k, h):
    if k == 2 and len(group) == 5:
        return group[2 + h]
    return group[k if k < 3 else len(group) - 1].at[h]


def input_kernel(y_ref, gu_ref, *refs):
    group, (own, other) = refs[:-2], refs[-2:]
    for h, out in ((0, own), (1, other)):
        total = None
        for k in range(NY):
            block = lax.rem(y_ref[0] + NY - k, NY)
            term = dot(delta_at(group, k, h)[: gu_ref.shape[1]], gu_ref[block], TN)
            total = term if total is None else total + term
        out[...] = total.astype(out.dtype)


def grads_kernel(first, layout, y_ref, *refs):
    n_out = 1 if first else 3
    ins, outs = list(refs[:-n_out]), refs[-n_out:]
    before = None if first else ins.pop(0)
    rows = (outs[0].shape[1] // 3) if first else outs[0].shape[1]
    groups = []
    for n_chunks, n_parts in layout:
        halves = [(ins.pop(0), ins.pop(0)) for _ in range(n_chunks)]
        groups.append((halves, [ins.pop(0) for _ in range(n_parts)]))
    for k in range(NY):
        block = lax.rem(y_ref[0] + NY - k, NY)
        gate_up, dn = None, None
        for halves, group in groups:
            for h in range(2):
                d = delta_at(group, k, h)
                at = 0
                for pair in halves:
                    tokens = slice(at, at + pair[h].shape[1])
                    at = tokens.stop
                    t = dot(d[: 2 * rows, tokens], pair[h][0], NN)
                    gate_up = t if gate_up is None else gate_up + t
                    t = dot(d[2 * rows :, tokens], pair[h][1], NN)
                    dn = t if dn is None else dn + t
        if first:
            outs[0][k, : 2 * rows] = gate_up
            outs[0][k, 2 * rows :] = dn
        else:
            gate_up = gate_up + before[k, : 2 * rows]
            dn = dn + before[k, 2 * rows :]
            for out, value in zip(outs, (gate_up[:rows], gate_up[rows:], dn)):
                out[block] = value.astype(out.dtype)


def per_device(activations, cotangent, gate_weight, up_weight, down_weight):
    y = lax.rem(lax.axis_index("row"), NY)[None].astype(jnp.int32)
    rows, feats = activations.shape
    hid = gate_weight.shape[1]
    hb = hid // NY
    shape = (NY, hb, feats)
    gate_up_w = jnp.concatenate([gate_weight.T.reshape(shape), up_weight.T.reshape(shape)], axis=1)
    down_w = down_weight.reshape(shape)
    line = Line()
    zh_tokens = NZH * rows
    n = len(CHUNKS)

    both = jnp.stack([activations, cotangent])
    gathered = [both] + [shift_col(both, dzh=k) for k in range(1, NZH)]
    source = line.call(functools.partial(pack_kernel, False), gathered, [sds((2, zh_tokens, feats), BF16)], 0, "pack_zh")[0]
    moved, halves, sent, sums, other_sums, groups = {0: source}, {}, {}, {}, {}, {}
    inputs, parts, final = {}, [], None

    def fetch_x(i, source):
        for s in CHUNKS[i]:
            if s not in moved:
                moved[s] = shift_col(source, dx=s)

    for what in ORDER:
        kind, i = what[0], int(what[1:] or 0)
        th = len(CHUNKS[i]) * zh_tokens if kind in "fso" else 0
        if kind == "f":
            pieces = [moved[s] for s in CHUNKS[i]]
            own = pieces[0]
            if len(pieces) > 1 or 0 < i < n - 1:
                out = [sds((2, th, feats), BF16)] + [sds(source.shape, BF16)] * (i < n - 1)
                res = line.call(functools.partial(pack_kernel, i < n - 1), pieces + [source] * (i < n - 1), out, 0, f"pack_x{i}")
                own, source = res[0], res[-1]
            halves[i] = (own, shift_col(own, dc=1))
            if i < n - 1:
                fetch_x(i + 1, source)
        elif kind == "s":
            ins = [gate_up_w, down_w, *halves[i]]
            out = [sds((2, 3 * hb, th), BF16)] * 3
            res = line.call(sent_kernel, ins, out, 2 * 9 * hb * 2 * th * feats, f"sent{i}", (y,))
            sent[i] = [shift_y(v, k) for v, k in zip(res, (2, 1, -1))]
        elif kind == "o":
            ins = [gate_up_w, down_w, *halves[i], *sent[i]]
            out = [sds((2, 3 * hb, th), F32)]
            if ZL_DTYPE[i] != F32:
                out.append(sds((2, 3 * hb, th), ZL_DTYPE[i]))
            after = [other_sums[j] for j in ZL_AHEAD.get(i, ())]
            res = line.call(own_kernel, ins, out, 2 * 3 * hb * 2 * th * feats, f"own{i}", (y,), after)
            sums[i], other_sums[i] = res[0], swap_zl(res[-1])
        elif kind == "d":
            ins = sum([[sums[j], other_sums[j]] for j in GROUPS[i]], [])
            th = sum(v.shape[2] for v in ins[::2])
            d0 = line.call(delta_kernel, ins, [sds((2, 3 * hb, th), BF16)], 0, f"delta{i}")[0]
            d1, d3 = shift_y(d0, 1), shift_y(d0, -1)
            if AG_RING[i]:
                groups[i] = (d0, d1, shift_y(d1[0], 1), shift_y(d3[1], -1), d3)
            else:
                groups[i] = (d0, d1, shift_y(d0, 2), d3)
        elif kind == "i":
            ins = [gate_up_w, *groups[i]]
            th = groups[i][0].shape[2]
            after = [groups[j][-1] for j in AHEAD.get(i, ())]
            out = [sds((th, feats), F32)] * 2
            keep, send = line.call(input_kernel, ins, out, 2 * 4 * hid * th * feats, f"input{i}", (y,), after)
            inputs[i] = (keep, shift_col(send, dc=1))
        elif kind == "p":
            shifts = sum([CHUNKS[j] for j in GROUPS[i]], ())
            out = [sds((zh_tokens, feats), BF16 if s else F32) for s in shifts]
            res = line.call(pair_kernel, inputs[i], out, 0, f"pair{i}")
            parts += [shift_col(v, dx=-s) if s else v for v, s in zip(res, shifts)]
        elif kind == "t":
            parts = [line.call(sum_kernel, parts, [sds((zh_tokens, feats), F32)], 0, "input_early")[0]]
        elif kind == "z":
            out = [sds((rows, feats), F32)] + [sds((rows, feats), ZH_DTYPE)] * (NZH - 1)
            res = line.call(total_kernel, parts, out, 0, "input_total")
            final = res[0]
            for k in range(1, NZH):
                final = final + shift_col(res[k], dzh=-k).astype(F32)
        elif kind in "vw":
            ins, layout = ([early_grads] if kind == "w" else []), []
            for j in LATE_GROUPS if kind == "w" else EARLY_GROUPS:
                for c in GROUPS[j]:
                    ins += halves[c]
                ins += groups[j]
                layout.append((len(GROUPS[j]), len(groups[j])))
            flops = 2 * 3 * NZH * NX * 2 * rows * hid * feats
            out = [sds(shape, BF16)] * 3 if kind == "w" else [sds((NY, 3 * hb, feats), F32)]
            res = line.call(functools.partial(grads_kernel, kind == "v", layout), ins, out, flops, f"grads_{kind}", (y,))
            if kind == "v":
                early_grads = res[0]
            else:
                gate_grad, up_grad, down_grad = res
    return (
        final.astype(BF16),
        gate_grad.reshape(hid, feats).T,
        up_grad.reshape(hid, feats).T,
        down_grad.reshape(hid, feats),
    )


def solution(mesh):
    return jax.shard_map(
        per_device,
        mesh=mesh,
        in_specs=(P("col", "row"), P("col", "row"), P("row", "col"), P("row", "col"), P("col", "row")),
        out_specs=(P("col", "row"), P("row", "col"), P("row", "col"), P("col", "row")),
        check_vma=False,
    )
```

```python
import functools

import jax
import jax.numpy as jnp
from jax import lax
from jax.experimental import pallas as pl
from jax.experimental.pallas import tpu as pltpu
from jax.sharding import PartitionSpec as P


BF16, F32 = jnp.bfloat16, jnp.float32
NY, NZH, NX = 4, 4, 4
CHUNKS = ((0,), (1, 3), (2,))
GROUPS = ((0,), (1,), (2,))
EARLY_GROUPS, LATE_GROUPS = (1, 2), (0,)
AHEAD = {1: (2,), 2: (0,)}
ZL_AHEAD = {1: (0,)}
AG_RING = (False, True, False)
ZL_DTYPE = (F32, BF16, BF16)
VMEM_MB = 10
ORDER = (
    "f0", "s0", "f1", "o0", "s1", "f2", "o1", "s2", "d1", "o2",
    "d2", "d0", "i1", "i2", "p1", "i0", "p2", "p0", "v", "t",
    "z", "w",
)
ZH_DTYPE = BF16

NT = (((1,), (1,)), ((), ()))
NN = (((1,), (0,)), ((), ()))
TN = (((0,), (0,)), ((), ()))


def dot(a, b, dims):
    return lax.dot_general(a, b, dims, preferred_element_type=F32)


def shift_y(v, k):
    return lax.ppermute(v, "row", [(z * NY + y, z * NY + (y + k) % NY) for z in range(2) for y in range(NY)])


def swap_zl(v):
    return lax.ppermute(v, "row", [(r, (r + NY) % (2 * NY)) for r in range(2 * NY)])


def shift_col(v, dzh=0, dx=0, dc=0):
    pairs = []
    for zh in range(NZH):
        for x in range(NX):
            for c in range(2):
                at = (zh * NX + x) * 2 + c
                to = (((zh + dzh) % NZH) * NX + (x + dx) % NX) * 2 + (c + dc) % 2
                pairs.append((at, to))
    return lax.ppermute(v, "col", pairs)


HEAVY = 10e9
LONG = ("own", "input0", "input2")


def cost(flops, bytes_accessed):
    return pl.CostEstimate(flops=int(flops), bytes_accessed=int(bytes_accessed), transcendentals=0)


def nbytes(*arrays):
    return sum(a.size * a.dtype.itemsize for a in arrays)


class Line:
    def __init__(self):
        self.last = None

    def call(self, kernel, inputs, outs, flops, name, scalars=(), after=(), vmem=VMEM_MB):
        flops = HEAVY if name.startswith(LONG) else 0
        after = list(after) + ([self.last] if self.last is not None else [])
        n_s, n_a = len(scalars), len(after)

        def run(*refs):
            kernel(*refs[:n_s], *refs[n_s + n_a :])

        vm = pl.BlockSpec(memory_space=pltpu.VMEM)
        res = pl.pallas_call(
            run,
            out_shape=outs,
            in_specs=[pl.BlockSpec(memory_space=pltpu.SMEM)] * n_s + [pl.BlockSpec(memory_space=pl.ANY)] * n_a + [vm] * len(inputs),
            out_specs=[vm] * len(outs),
            compiler_params=pltpu.CompilerParams(vmem_limit_bytes=vmem * 2**20),
            cost_estimate=cost(flops, 0),
            name=name,
        )(*scalars, *after, *inputs)
        self.last = res[0]
        return res


def sds(shape, dtype):
    return jax.ShapeDtypeStruct(shape, dtype)


def pack_kernel(copied, *refs):
    ins, outs = refs[: -1 - copied], refs[-1 - copied :]
    if copied:
        outs[1][...] = ins[-1][...]
        ins = ins[:-1]
    at = 0
    for r in ins:
        size = r.shape[1]
        outs[0][:, at : at + size] = r[...]
        at += size


def pair_kernel(keep, got, *outs):
    rows = outs[0].shape[0]
    for j, out in enumerate(outs):
        at = slice(j * rows, (j + 1) * rows)
        out[...] = (keep[at] + got[at]).astype(out.dtype)


def sum_kernel(*refs):
    total = refs[0][...].astype(F32)
    for p in refs[1:-1]:
        total = total + p[...].astype(F32)
    refs[-1][...] = total


def total_kernel(*refs):
    parts, outs = refs[: -NZH], refs[-NZH:]
    rows = outs[0].shape[0]
    for k, out in enumerate(outs):
        at = slice(k * rows, (k + 1) * rows)
        total = parts[0][at].astype(F32)
        for p in parts[1:]:
            total = total + p[at].astype(F32)
        out[...] = total.astype(out.dtype)


def block_part(block, gu_ref, dn_ref, half):
    gate_up = dot(gu_ref[block], half[0], NT)
    down = dot(dn_ref[block], half[1], NT)
    return jnp.concatenate([gate_up, down], axis=0)


def sent_kernel(y_ref, gu_ref, dn_ref, own, other, *outs):
    for out, k in zip(outs, (2, 1, 3)):
        block = lax.rem(y_ref[0] + k, NY)
        for h, half in enumerate((own, other)):
            out[h] = block_part(block, gu_ref, dn_ref, half).astype(out.dtype)


def own_kernel(y_ref, gu_ref, dn_ref, own, other, a, b, c, out, *sent):
    for h, half in enumerate((own, other)):
        part = block_part(y_ref[0], gu_ref, dn_ref, half)
        part = part + a[h].astype(F32) + b[h].astype(F32) + c[h].astype(F32)
        out[h] = part
        for s in sent:
            s[h] = part.astype(s.dtype)


def delta_kernel(*refs):
    ins, out = refs[:-1], refs[-1]
    at = 0
    for mine, theirs in zip(ins[::2], ins[1::2]):
        rows, size = mine.shape[1] // 3, mine.shape[2]
        for h in range(2):
            sums = mine[h] + theirs[h].astype(F32)
            gate, up, hidden_grad = sums[:rows], sums[rows : 2 * rows], sums[2 * rows :]
            s = 1.0 / (1.0 + jnp.exp(-gate))
            silu = gate * s
            gate_delta = hidden_grad * up * s * (1.0 + gate * (1.0 - s))
            three = jnp.concatenate([gate_delta, hidden_grad * silu, silu * up], axis=0)
            out[h, :, at : at + size] = three.astype(out.dtype)
        at += size


def delta_at(group, k, h):
    if k == 2 and len(group) == 5:
        return group[2 + h]
    return group[k if k < 3 else len(group) - 1].at[h]


def input_kernel(y_ref, gu_ref, *refs):
    group, (own, other) = refs[:-2], refs[-2:]
    for h, out in ((0, own), (1, other)):
        total = None
        for k in range(NY):
            block = lax.rem(y_ref[0] + NY - k, NY)
            term = dot(delta_at(group, k, h)[: gu_ref.shape[1]], gu_ref[block], TN)
            total = term if total is None else total + term
        out[...] = total.astype(out.dtype)


def grads_kernel(first, layout, y_ref, *refs):
    n_out = 1 if first else 3
    ins, outs = list(refs[:-n_out]), refs[-n_out:]
    before = None if first else ins.pop(0)
    rows = (outs[0].shape[1] // 3) if first else outs[0].shape[1]
    groups = []
    for n_chunks, n_parts in layout:
        halves = [(ins.pop(0), ins.pop(0)) for _ in range(n_chunks)]
        groups.append((halves, [ins.pop(0) for _ in range(n_parts)]))
    for k in range(NY):
        block = lax.rem(y_ref[0] + NY - k, NY)
        gate_up, dn = None, None
        for halves, group in groups:
            for h in range(2):
                d = delta_at(group, k, h)
                at = 0
                for pair in halves:
                    tokens = slice(at, at + pair[h].shape[1])
                    at = tokens.stop
                    t = dot(d[: 2 * rows, tokens], pair[h][0], NN)
                    gate_up = t if gate_up is None else gate_up + t
                    t = dot(d[2 * rows :, tokens], pair[h][1], NN)
                    dn = t if dn is None else dn + t
        if first:
            outs[0][k, : 2 * rows] = gate_up
            outs[0][k, 2 * rows :] = dn
        else:
            gate_up = gate_up + before[k, : 2 * rows]
            dn = dn + before[k, 2 * rows :]
            for out, value in zip(outs, (gate_up[:rows], gate_up[rows:], dn)):
                out[block] = value.astype(out.dtype)


def per_device(activations, cotangent, gate_weight, up_weight, down_weight):
    y = lax.rem(lax.axis_index("row"), NY)[None].astype(jnp.int32)
    rows, feats = activations.shape
    hid = gate_weight.shape[1]
    hb = hid // NY
    shape = (NY, hb, feats)
    gate_up_w = jnp.concatenate([gate_weight.T.reshape(shape), up_weight.T.reshape(shape)], axis=1)
    down_w = down_weight.reshape(shape)
    line = Line()
    zh_tokens = NZH * rows
    n = len(CHUNKS)

    both = jnp.stack([activations, cotangent])
    gathered = [both] + [shift_col(both, dzh=k) for k in range(1, NZH)]
    source = line.call(functools.partial(pack_kernel, False), gathered, [sds((2, zh_tokens, feats), BF16)], 0, "pack_zh")[0]
    moved, halves, sent, sums, other_sums, groups = {0: source}, {}, {}, {}, {}, {}
    inputs, parts, final = {}, [], None

    def fetch_x(i, source):
        for s in CHUNKS[i]:
            if s not in moved:
                moved[s] = shift_col(source, dx=s)

    for what in ORDER:
        kind, i = what[0], int(what[1:] or 0)
        th = len(CHUNKS[i]) * zh_tokens if kind in "fso" else 0
        if kind == "f":
            pieces = [moved[s] for s in CHUNKS[i]]
            own = pieces[0]
            if len(pieces) > 1 or 0 < i < n - 1:
                out = [sds((2, th, feats), BF16)] + [sds(source.shape, BF16)] * (i < n - 1)
                res = line.call(functools.partial(pack_kernel, i < n - 1), pieces + [source] * (i < n - 1), out, 0, f"pack_x{i}")
                own, source = res[0], res[-1]
            halves[i] = (own, shift_col(own, dc=1))
            if i < n - 1:
                fetch_x(i + 1, source)
        elif kind == "s":
            ins = [gate_up_w, down_w, *halves[i]]
            out = [sds((2, 3 * hb, th), BF16)] * 3
            res = line.call(sent_kernel, ins, out, 2 * 9 * hb * 2 * th * feats, f"sent{i}", (y,))
            sent[i] = [shift_y(v, k) for v, k in zip(res, (2, 1, -1))]
        elif kind == "o":
            ins = [gate_up_w, down_w, *halves[i], *sent[i]]
            out = [sds((2, 3 * hb, th), F32)]
            if ZL_DTYPE[i] != F32:
                out.append(sds((2, 3 * hb, th), ZL_DTYPE[i]))
            after = [other_sums[j] for j in ZL_AHEAD.get(i, ())]
            res = line.call(own_kernel, ins, out, 2 * 3 * hb * 2 * th * feats, f"own{i}", (y,), after)
            sums[i], other_sums[i] = res[0], swap_zl(res[-1])
        elif kind == "d":
            ins = sum([[sums[j], other_sums[j]] for j in GROUPS[i]], [])
            th = sum(v.shape[2] for v in ins[::2])
            d0 = line.call(delta_kernel, ins, [sds((2, 3 * hb, th), BF16)], 0, f"delta{i}")[0]
            d1, d3 = shift_y(d0, 1), shift_y(d0, -1)
            if AG_RING[i]:
                groups[i] = (d0, d1, shift_y(d1[0], 1), shift_y(d3[1], -1), d3)
            else:
                groups[i] = (d0, d1, shift_y(d0, 2), d3)
        elif kind == "i":
            ins = [gate_up_w, *groups[i]]
            th = groups[i][0].shape[2]
            after = [v for j in AHEAD.get(i, ()) for v in groups[j][-1 if i == 1 else 1 :]]
            out = [sds((th, feats), F32)] * 2
            keep, send = line.call(input_kernel, ins, out, 2 * 4 * hid * th * feats, f"input{i}", (y,), after)
            inputs[i] = (keep, shift_col(send, dc=1))
        elif kind == "p":
            shifts = sum([CHUNKS[j] for j in GROUPS[i]], ())
            out = [sds((zh_tokens, feats), BF16 if s else F32) for s in shifts]
            res = line.call(pair_kernel, inputs[i], out, 0, f"pair{i}")
            parts += [shift_col(v, dx=-s) if s else v for v, s in zip(res, shifts)]
        elif kind == "t":
            parts = [line.call(sum_kernel, parts, [sds((zh_tokens, feats), F32)], 0, "input_early")[0]]
        elif kind == "z":
            out = [sds((rows, feats), F32)] + [sds((rows, feats), ZH_DTYPE)] * (NZH - 1)
            res = line.call(total_kernel, parts, out, 0, "input_total")
            final = res[0]
            for k in range(1, NZH):
                final = final + shift_col(res[k], dzh=-k).astype(F32)
        elif kind in "vw":
            ins, layout = ([early_grads] if kind == "w" else []), []
            for j in LATE_GROUPS if kind == "w" else EARLY_GROUPS:
                for c in GROUPS[j]:
                    ins += halves[c]
                ins += groups[j]
                layout.append((len(GROUPS[j]), len(groups[j])))
            flops = 2 * 3 * NZH * NX * 2 * rows * hid * feats
            out = [sds(shape, BF16)] * 3 if kind == "w" else [sds((NY, 3 * hb, feats), F32)]
            res = line.call(functools.partial(grads_kernel, kind == "v", layout), ins, out, flops, f"grads_{kind}", (y,))
            if kind == "v":
                early_grads = res[0]
            else:
                gate_grad, up_grad, down_grad = res
    return (
        final.astype(BF16),
        gate_grad.reshape(hid, feats).T,
        up_grad.reshape(hid, feats).T,
        down_grad.reshape(hid, feats),
    )


def solution(mesh):
    return jax.shard_map(
        per_device,
        mesh=mesh,
        in_specs=(P("col", "row"), P("col", "row"), P("row", "col"), P("row", "col"), P("col", "row")),
        out_specs=(P("col", "row"), P("row", "col"), P("row", "col"), P("col", "row")),
        check_vma=False,
    )
```
